32 devices in a mesh: doc: 8 (over z, y), head: 4 (over x, core).
Axes of the slice: x: 2, y: 2, z: 4, core: 2. Of those that a mesh axis runs over, the one named last changes fastest.
Arguments:
- target_q: bfloat16 [1024, 2048], P('doc', 'head'), may hold values from -300 to 300
- target_kv: bfloat16 [1024, 512], P('doc', 'head'), may hold values from -8 to 8
- doc_kv: bfloat16 [8, 384, 512], P('doc', None, 'head'), may hold values from -6 to 6
- doc_lengths: int32 [8], replicated, may hold values from 1 to 384, 2304 in all
- segment_ids: int32 [1024], replicated, may hold values from 0 to 15, never falling along the last dimension, each value on 1 to 128 neighbouring positions
- out_weight: bfloat16 [2048, 8192], P('head', 'doc'), may hold values from -0.125 to 0.125
Outputs:
- projected: bfloat16 [1024, 8192], P('head', 'doc')
The draws below stay inside these ranges and needn't reach their ends.
Inputs may be any that keep to these rules, and one draw needn't show every extreme that they name: `segment_ids`: segment numbers never fall along the target rows, and each segment spans at most 128 rows.
All inputs are finite; a program needn't handle non-finite values.
Results may differ from the reference program's by a relative error of at most 0.005.
Values may be sent and summed in bfloat16 or wider, within the bound.
A program may use at most 64 MiB of HBM per device.

```python
import math
import jax
import jax.numpy as jnp
import numpy as np
from jax import lax

D = 8192
HD = 128
GROUP = 8
TQ_DEV = 128
DOC_LEN = 384
NDOC = 8
HEADS = 16
KVH = 2
TARGET = 1024


def anchor_keys(key):
    return jnp.clip(jax.random.normal(jax.random.fold_in(key, 12), (NDOC, KVH, HD), jnp.float32), -6.0, 6.0)


def draw_doc_kv(key, part):
    key_field = jnp.clip(jax.random.normal(jax.random.fold_in(key, 11), (NDOC, DOC_LEN, KVH, 2, HD), jnp.float32), -6.0, 6.0)
    anchor = anchor_keys(key)
    key_field = key_field.at[:, 0, :, 0, :].set(anchor)
    return key_field.reshape(NDOC, DOC_LEN, KVH * 2 * HD).astype(jnp.bfloat16)


def draw_target_q(key, part):
    queries = jnp.clip(2.0 * jax.random.normal(jax.random.fold_in(key, 21), (TARGET, HEADS, HD), jnp.float32), -12.0, 12.0)
    return queries.reshape(TARGET, HEADS * HD).astype(jnp.bfloat16)


def shard_levels(key, shape, split, low, largest):
    gain = 1.0
    for dim, shards_of in split:
        draws = jax.random.uniform(jax.random.fold_in(jax.random.fold_in(key, 6), dim), (shards_of,), jnp.float32, low / len(split), largest / len(split))
        gain = gain * jnp.repeat(jnp.exp(draws), shape[dim] // shards_of).reshape((-1,) + (1,) * (len(shape) - 1 - dim))
    return gain


def split_up(number_of, total, most, skew):
    loads = [(1 << 20) // math.isqrt(standing ** skew) + 1 for standing in range(2, number_of + 1)]
    surplus, holding = total - most - (number_of - 1), [1] * (number_of - 1)
    while surplus > 0:
        movable = [i for i in range(number_of - 1) if holding[i] < most]
        pool, budget = sum([loads[i] for i in movable]), surplus
        for i in movable:
            addition = min(most - holding[i], max(1, budget * loads[i] // pool), surplus)
            holding[i] = holding[i] + addition
            surplus = surplus - addition
    return np.array([most] + holding)


def ragged(rng, number_of, total, limit, slope):
    if number_of == 2:
        one = jax.random.randint(rng, (), max(1, total - limit), min(limit, total - 1) + 1)
        return jnp.stack([one, total - one])
    tallies = jnp.asarray(split_up(number_of, total, limit, slope), jnp.int32)
    pairs = (number_of - 1) // 2
    source_of, sink = tallies[1:1 + 2 * pairs:2], tallies[2:2 + 2 * pairs:2]
    margin = jnp.minimum(source_of - 1, limit - sink)
    moved = jax.random.randint(jax.random.fold_in(rng, 1), (pairs,), 0, 1 << 20) % (margin + 1)
    tallies = tallies.at[1:1 + 2 * pairs:2].set(source_of - moved).at[2:2 + 2 * pairs:2].set(sink + moved)
    return tallies[jax.random.permutation(jax.random.fold_in(rng, 2), number_of)]


def centred(own_key, dims, scale, bound, cuts=(), kind=jnp.bfloat16):
    gain = shard_levels(own_key, dims, cuts, -0.22, 0.18) if cuts else 1.0
    array = jax.random.normal(own_key, dims, jnp.float32) * scale * gain
    return jnp.minimum(jnp.maximum(array, -bound), bound).astype(kind)


def setup_inputs(seed: int = 0) -> dict:
    key_list = jax.random.split(jax.random.key(seed), 7)
    return {
        "target_q": draw_target_q(jax.random.fold_in(key_list[6], 71), 0),
        "target_kv": centred(key_list[1], (TARGET, KVH * 2 * HD), 2.0, 8.0, ((0, 8), (1, 4))),
        "doc_kv": draw_doc_kv(jax.random.fold_in(key_list[6], 71), 0),
        "doc_lengths": ragged(key_list[3], NDOC, NDOC * DOC_LEN * 3 // 4, DOC_LEN, 0).astype(jnp.int32),
        "segment_ids": jnp.searchsorted(jnp.cumsum(ragged(key_list[4], 2 * NDOC, TARGET, TQ_DEV, 0)), jnp.arange(TARGET), side="right").astype(jnp.int32),
        "out_weight": centred(key_list[5], (HEADS * HD, D), (HEADS * HD) ** -0.5, 0.125, ((0, 4), (1, 8))),
    }


masked_score = -1e+30

def block_stats(queries, key_block, value_block, visible):
    scaling = 1.0 / math.sqrt(HD)
    scores = jnp.einsum('tkgh,pkh->tkgp', queries, key_block.astype(jnp.float32)) * scaling
    scores = jnp.where(visible, scores, masked_score)
    highest = lax.optimization_barrier(jnp.max(scores, axis=-1))
    weights = jnp.exp(scores - highest[..., None])
    summed = lax.optimization_barrier(jnp.sum(weights, axis=-1))
    rounded = lax.optimization_barrier(weights.astype(jnp.bfloat16)).astype(jnp.float32)
    blended = jnp.einsum('tkgp,pkh->tkgh', rounded, value_block.astype(jnp.float32))
    return (highest, summed, blended)

def reference(target_q, target_kv, doc_kv, doc_lengths, segment_ids, out_weight):
    queries_all = target_q.astype(jnp.float32).reshape(NDOC, TQ_DEV, KVH, GROUP, HD)
    target_pairs = target_kv.reshape(NDOC, TQ_DEV, KVH, 2, HD)
    doc_pairs = doc_kv.reshape(NDOC, DOC_LEN, KVH, 2, HD)
    seg_blocks = segment_ids.reshape(NDOC, TQ_DEV)
    slot_index = jnp.arange(DOC_LEN, dtype=jnp.int32)
    token_pos = jnp.arange(TQ_DEV, dtype=jnp.int32)

    def row_block(block_id):
        queries = lax.dynamic_index_in_dim(queries_all, block_id, 0, keepdims=False)

        def doc_stats(doc_id):
            pair = lax.dynamic_index_in_dim(doc_pairs, doc_id, 0, keepdims=False)
            length = lax.dynamic_index_in_dim(doc_lengths, doc_id, 0, keepdims=False)
            visible = (slot_index < length)[None, None, None, :]
            return block_stats(queries, pair[:, :, 0, :], pair[:, :, 1, :], visible)
        doc_high, doc_sum, doc_out = lax.map(doc_stats, jnp.arange(NDOC, dtype=jnp.int32))
        prev_id = jnp.maximum(block_id - 1, 0).astype(jnp.int32)
        own_seg = lax.dynamic_index_in_dim(seg_blocks, block_id, 0, keepdims=False)
        prev_seg = jnp.where(block_id > 0, lax.dynamic_index_in_dim(seg_blocks, prev_id, 0, keepdims=False), -1)
        own_pair = lax.dynamic_index_in_dim(target_pairs, block_id, 0, keepdims=False)
        prev_pair = lax.dynamic_index_in_dim(target_pairs, prev_id, 0, keepdims=False)
        own_vis = ((own_seg[:, None] == own_seg[None, :]) & (token_pos[None, :] <= token_pos[:, None]))[:, None, None, :]
        prev_vis = (own_seg[:, None] == prev_seg[None, :])[:, None, None, :]
        own_high, own_sum, own_out = block_stats(queries, own_pair[:, :, 0, :], own_pair[:, :, 1, :], own_vis)
        prev_high, prev_sum, prev_out = block_stats(queries, prev_pair[:, :, 0, :], prev_pair[:, :, 1, :], prev_vis)
        highs = jnp.concatenate([doc_high, own_high[None], prev_high[None]], axis=0)
        sums = jnp.concatenate([doc_sum, own_sum[None], prev_sum[None]], axis=0)
        outs = jnp.concatenate([doc_out, own_out[None], prev_out[None]], axis=0)
        overall = lax.optimization_barrier(jnp.max(highs, axis=0))
        factor = jnp.exp(highs - overall[None])
        summed = lax.optimization_barrier(jnp.sum(factor * sums, axis=0))
        blended = lax.optimization_barrier(jnp.sum(factor[..., None] * outs, axis=0))
        return (blended / summed[..., None]).astype(jnp.bfloat16).reshape(TQ_DEV, HEADS * HD)
    attention = lax.map(row_block, jnp.arange(NDOC, dtype=jnp.int32)).reshape(TARGET, HEADS * HD)
    return jnp.dot(attention, out_weight, preferred_element_type=jnp.float32).astype(jnp.bfloat16)
```

```python
import math

import jax
import jax.numpy as jnp
from jax import lax
from jax.experimental import pallas as pl
from jax.experimental.pallas import tpu as pltpu
from jax.sharding import PartitionSpec as P

MASKED = -1e30
F32 = jnp.float32
BF16 = jnp.bfloat16


def ordered(pos, count, k):
    right = count - 1 - pos
    both = jnp.minimum(pos, right)
    near = jnp.where(k % 2 == 1, (k + 1) // 2, -(k // 2))
    far = jnp.where(right > pos, k - both, both - k)
    return pos + jnp.where(k <= 2 * both, near, far)


def kernel(
    ndoc,
    nhead,
    q_ref,
    tkv_ref,
    dkv_ref,
    len_ref,
    seg_ref,
    w_ref,
    out_ref,
    kv,
    tkv,
    wbuf,
    qbuf,
    m_s,
    l_s,
    acc_s,
    att,
    abuf,
    own,
    sbuf,
    rbuf,
    s_z,
    s_y,
    s_sib,
    r_doc,
    r_sib,
    s_t,
    r_t,
    s_w,
    r_w,
    l_w,
    s_a,
    s_az,
    s_ay,
    r_a,
    s_p,
    r_p,
):
    rows = q_ref.shape[0]
    hd = tkv_ref.shape[1]
    heads = q_ref.shape[1] // hd
    cols = q_ref.shape[1]
    Z = ndoc // 2
    PAIRS = nhead // 2
    me = lax.axis_index("doc")
    hi = lax.axis_index("head")
    zi, y = me // 2, me % 2
    p, c = hi // 2, hi % 2
    sib = 2 * p + 1 - c
    ynb = 2 * zi + 1 - y
    t = zi % 2
    owner = 2 * p + t
    has_l, has_r = zi > 0, zi < Z - 1
    has_prev, has_next = me > 0, me < ndoc - 1
    coef = math.log2(math.e) / math.sqrt(hd)

    def rc(src, dst, ss, rs, doc, head):
        return pltpu.make_async_remote_copy(
            src_ref=src,
            dst_ref=dst,
            send_sem=ss,
            recv_sem=rs,
            device_id={"doc": doc, "head": head},
            device_id_type=pl.DeviceIdType.MESH,
        )

    barrier = pltpu.get_barrier_semaphore()

    def greet(doc, head):
        pl.semaphore_signal(
            barrier, inc=1, device_id={"doc": doc, "head": head}, device_id_type=pl.DeviceIdType.MESH
        )

    diag = jnp.where(y == 1, me + 1, me - 1)
    has_diag = ((y == 1) & has_r) | ((y == 0) & has_l)
    greet(me, sib)
    for core in range(2):
        greet(ynb, 2 * p + core)

        @pl.when(has_l)
        def _():
            greet(me - 2, 2 * p + core)

        @pl.when(has_r)
        def _():
            greet(me + 2, 2 * p + core)

        @pl.when(has_diag)
        def _():
            greet(diag, 2 * p + core)

    for k in range(1, PAIRS):
        greet(me, 2 * ((p + k) % PAIRS) + c)
    sides = sum(cond.astype(jnp.int32) for cond in (has_l, has_r, has_diag))
    pl.semaphore_wait(barrier, 2 + PAIRS + 2 * sides)

    def send_r(src, doc):
        return rc(src, kv.at[c, doc], s_z.at[doc], r_doc.at[doc], me + 2, hi)

    def send_l(src, doc):
        return rc(src, kv.at[c, doc], s_z.at[doc], r_doc.at[doc], me - 2, hi)

    s_l0 = s_w.at[1]

    def send_l0(src, doc):
        return rc(src, kv.at[c, doc], s_l0, r_doc.at[doc], me - 2, hi)

    def send_y(src, doc):
        return rc(src, kv.at[c, doc], s_y.at[doc], r_doc.at[doc], ynb, hi)

    def send_sib(src, doc):
        return rc(src, kv.at[c, doc], s_sib.at[doc], r_sib.at[doc], me, sib)

    own_block = dkv_ref.at[0]
    t_own = rc(tkv_ref, tkv.at[c, pl.ds(rows, rows)], s_t.at[0], r_t.at[1], me, sib)
    t_next = [
        rc(tkv_ref, tkv.at[c, pl.ds(0, rows)], s_t.at[1], r_t.at[2], me + 1, hi),
        rc(tkv_ref, tkv.at[c, pl.ds(0, rows)], s_t.at[2], r_t.at[0], me + 1, sib),
    ]
    t_own.start()
    pl.when(has_r)(lambda: send_r(own_block, me).start())
    pl.when(has_l)(lambda: send_l0(own_block, me).start())
    send_y(own_block, me).start()
    send_sib(own_block, me).start()

    @pl.when(has_next)
    def _():
        t_next[0].start()
        t_next[1].start()

    w_local = pltpu.make_async_copy(w_ref, wbuf.at[c], l_w)
    w_remote = rc(w_ref, wbuf.at[c], s_w.at[0], r_w, me, sib)
    w_local.start()
    w_remote.start()

    kv[c, me] = dkv_ref[0]
    tkv[c, pl.ds(rows, rows)] = tkv_ref[...]
    for j in range(heads):
        qbuf[j * rows : (j + 1) * rows] = q_ref[:, j * hd : (j + 1) * hd]

    @pl.when(me == 0)
    def _():
        tkv[:, pl.ds(0, rows)] = jnp.zeros((2, rows, hd), BF16)

    def attend(keys, values, mask_of, first):
        half = cols // 2
        for part in range(2):
            at = slice(part * half, (part + 1) * half)
            scores = lax.dot_general(
                keys, qbuf[at], (((1,), (1,)), ((), ())), preferred_element_type=F32
            )
            scores = jnp.where(mask_of(half), scores, MASKED)
            high = jnp.max(scores, axis=0, keepdims=True)
            if not first:
                before = m_s[:, at]
                high = jnp.maximum(high, before)
            weights = jnp.exp2((scores - high) * coef)
            total = jnp.sum(weights, axis=0, keepdims=True)
            blended = lax.dot_general(
                values,
                weights.astype(BF16),
                (((0,), (0,)), ((), ())),
                preferred_element_type=F32,
            )
            if not first:
                factor = jnp.exp2((before - high) * coef)
                total = total + factor * l_s[:, at]
                blended = blended + factor * acc_s[:, at]
            m_s[:, at] = high
            l_s[:, at] = total
            acc_s[:, at] = blended

    own_row = seg_ref[pl.ds(me, 1), :]
    prev_row = seg_ref[pl.ds(jnp.maximum(me - 1, 0), 1), :]

    def column(row):
        return jnp.broadcast_to(row.astype(F32), (rows, rows)).T

    own_col, prev_col = column(own_row), column(prev_row)
    own_rowf = jnp.broadcast_to(own_row.astype(F32), (rows, rows))
    key_pos = lax.broadcasted_iota(jnp.int32, (rows, rows), 0)
    row_pos = lax.broadcasted_iota(jnp.int32, (rows, rows), 1)
    prev_mask = jnp.where(has_prev, (prev_col == own_rowf).astype(F32), 0.0)
    own_mask = jnp.where((own_col == own_rowf) & (key_pos <= row_pos), 1.0, 0.0)
    tmask = jnp.concatenate([prev_mask, own_mask], axis=0)

    t_own.wait_recv()

    @pl.when(has_prev)
    def _():
        t_next[0].wait_recv()
        t_next[1].wait_recv()

    attend(
        tkv[0],
        tkv[1],
        lambda n: jnp.concatenate([tmask] * (n // rows), axis=1) > 0.5,
        True,
    )

    def attend_doc(doc):
        send_sib(own_block, doc).wait_recv()
        keys = kv[0, doc]
        length = len_ref[doc]

        def mask_of(n):
            return lax.broadcasted_iota(jnp.int32, (keys.shape[0], n), 0) < length

        attend(keys, kv[1, doc], mask_of, False)

    def doc_step(i, _):
        @pl.when(i < Z)
        def _():
            z = ordered(zi, Z, i)
            doc = 2 * z + y
            block = kv.at[c, doc]
            send_y(own_block, doc).wait_recv()
            pl.when((z < zi) & has_r)(lambda: send_r(block, doc).start())
            pl.when((z > zi) & has_l)(lambda: send_l(block, doc).start())
            send_y(block, doc).start()
            send_sib(block, doc).start()

        z = ordered(zi, Z, i - 1)
        other = 2 * z + 1 - y
        send_y(own_block, other).wait_recv()
        send_sib(kv.at[c, other], other).start()
        attend_doc(2 * z + y)
        attend_doc(other)
        return 0

    lax.fori_loop(1, Z + 1, doc_step, 0)

    for j in range(heads):
        at = slice(j * rows, (j + 1) * rows)
        att[:, at] = (acc_s[:, at] / l_s[:, at]).T.astype(BF16)

    def unit(z, yy, half):
        return abuf.at[z // 2, yy, half]

    a_sib = rc(att, unit(zi, y, c), s_a.at[0], r_a.at[zi // 2, y, c], me, sib)
    a_r = rc(att, unit(zi, y, c), s_a.at[1], r_a.at[zi // 2, y, c], me + 2, owner)
    a_l = rc(att, unit(zi, y, c), s_a.at[2], r_a.at[zi // 2, y, c], me - 2, owner)
    a_y = rc(att, unit(zi, y, c), s_a.at[3], r_a.at[zi // 2, y, c], ynb, owner)
    pl.when(has_r)(lambda: a_r.start())
    pl.when(has_l)(lambda: a_l.start())
    a_y.start()
    pl.when(t != c)(lambda: a_sib.start())

    @pl.when(t == c)
    def _():
        abuf[zi // 2, y, c] = att[...]

    w_local.wait()
    w_remote.wait_recv()

    def fwd(z, half, doc, sems):
        return rc(
            unit(z, y, half),
            unit(z, y, half),
            sems.at[z // 2, half],
            r_a.at[z // 2, y, half],
            doc,
            hi,
        )

    def arrived(z, yy, half):
        rc(
            unit(z, yy, half), unit(z, yy, half), s_a.at[0], r_a.at[z // 2, yy, half], ynb, hi
        ).wait_recv()

    def part_copy(z, yy):
        return rc(sbuf.at[z // 2, yy], rbuf.at[p, yy], s_p.at[z // 2, yy], r_p.at[p, yy], me, z)

    def project(z, yy):
        part = jnp.dot(abuf[z // 2, yy, 0], wbuf[0], preferred_element_type=F32)
        part = part + jnp.dot(abuf[z // 2, yy, 1], wbuf[1], preferred_element_type=F32)

        @pl.when(z // 2 == p)
        def _():
            own[yy] = part

        @pl.when(z // 2 != p)
        def _():
            sbuf[z // 2, yy] = part.astype(BF16)
            part_copy(z, yy).start()

    def place(k):
        return 2 * ordered(zi // 2, Z // 2, k) + c

    def proj_step(k, _):
        @pl.when(k < Z // 2)
        def _():
            z = place(k)

            @pl.when(z == zi)
            def _():
                arrived(z, y, 1 - c)

            for half in range(2):

                @pl.when(z != zi)
                def _():
                    arrived(z, y, half)
                    fwd(z, half, ynb, s_ay).start()

                pl.when((z < zi) & has_r)(lambda: fwd(z, half, me + 2, s_az).start())
                pl.when((z > zi) & has_l)(lambda: fwd(z, half, me - 2, s_az).start())
            project(z, y)

        @pl.when(k > 0)
        def _():
            z = place(k - 1)
            arrived(z, 1 - y, 0)
            arrived(z, 1 - y, 1)
            project(z, 1 - y)

        return 0

    lax.fori_loop(0, Z // 2 + 1, proj_step, 0)

    def add_in(k, _):
        src = (p + k) % PAIRS
        for yy in range(2):
            rc(sbuf.at[src, yy], rbuf.at[src, yy], s_p.at[src, yy], r_p.at[src, yy], me, hi_of(src)).wait_recv()
            own[yy] = own[yy] + rbuf[src, yy].astype(F32)
        return 0

    def hi_of(src):
        return 2 * src + c

    if PAIRS == 2:
        src = 1 - p
        for yy in range(2):
            rc(sbuf.at[src, yy], rbuf.at[src, yy], s_p.at[src, yy], r_p.at[src, yy], me, hi_of(src)).wait_recv()
            out_ref[yy * rows : (yy + 1) * rows] = (own[yy] + rbuf[src, yy].astype(F32)).astype(BF16)
    else:
        lax.fori_loop(1, PAIRS, add_in, 0)
        for yy in range(2):
            out_ref[yy * rows : (yy + 1) * rows] = own[yy].astype(BF16)

    t_own.wait_send()

    @pl.when(has_next)
    def _():
        t_next[0].wait_send()
        t_next[1].wait_send()

    pl.when(has_r)(lambda: send_r(own_block, me).wait_send())
    pl.when(has_l)(lambda: send_l0(own_block, me).wait_send())
    w_remote.wait_send()

    def drain(z, _):
        doc = 2 * z + y
        send_y(own_block, doc).wait_send()
        send_sib(own_block, doc).wait_send()
        send_sib(own_block, 2 * z + 1 - y).wait_send()
        pl.when((z < zi) & has_r)(lambda: send_r(own_block, doc).wait_send())
        pl.when((z > zi) & has_l)(lambda: send_l(own_block, doc).wait_send())

        @pl.when(z % 2 == c)
        def _():
            for half in range(2):
                pl.when(z != zi)(lambda: fwd(z, half, ynb, s_ay).wait_send())
                pl.when((z < zi) & has_r)(lambda: fwd(z, half, me + 2, s_az).wait_send())
                pl.when((z > zi) & has_l)(lambda: fwd(z, half, me - 2, s_az).wait_send())

            @pl.when(z // 2 != p)
            def _():
                for yy in range(2):
                    part_copy(z, yy).wait_send()

        return 0

    lax.fori_loop(0, Z, drain, 0)
    pl.when(has_r)(lambda: a_r.wait_send())
    pl.when(has_l)(lambda: a_l.wait_send())
    a_y.wait_send()
    pl.when(t != c)(lambda: a_sib.wait_send())


def body(target_q, target_kv, doc_kv, doc_lengths, segment_ids, out_weight, ndoc, nhead):
    rows, cols = target_q.shape
    hd = target_kv.shape[1]
    slots = doc_kv.shape[1]
    wide = out_weight.shape[1]
    Z, pairs = ndoc // 2, nhead // 2
    vmem = pl.BlockSpec(memory_space=pltpu.VMEM)
    dma = pltpu.SemaphoreType.DMA
    flops = 4 * rows * cols * (ndoc * slots + 2 * rows) + 2 * ndoc * rows * cols * wide
    return pl.pallas_call(
        lambda *refs: kernel(ndoc, nhead, *refs),
        out_shape=jax.ShapeDtypeStruct((2 * rows, wide), BF16),
        in_specs=[
            vmem,
            vmem,
            vmem,
            pl.BlockSpec(memory_space=pltpu.SMEM),
            vmem,
            pl.BlockSpec(memory_space=pl.ANY),
        ],
        out_specs=vmem,
        scratch_shapes=[
            pltpu.VMEM((2, ndoc, slots, hd), BF16),
            pltpu.VMEM((2, 2 * rows, hd), BF16),
            pltpu.VMEM((2, cols, wide), BF16),
            pltpu.VMEM((cols // hd * rows, hd), BF16),
            pltpu.VMEM((1, cols // hd * rows), F32),
            pltpu.VMEM((1, cols // hd * rows), F32),
            pltpu.VMEM((hd, cols // hd * rows), F32),
            pltpu.VMEM((rows, cols), BF16),
            pltpu.VMEM((Z // 2, 2, 2, rows, cols), BF16),
            pltpu.VMEM((2, rows, wide), F32),
            pltpu.VMEM((pairs, 2, rows, wide), BF16),
            pltpu.VMEM((pairs, 2, rows, wide), BF16),
            dma((ndoc,)),
            dma((ndoc,)),
            dma((ndoc,)),
            dma((ndoc,)),
            dma((ndoc,)),
            dma((3,)),
            dma((3,)),
            dma((2,)),
            dma,
            dma,
            dma((4,)),
            dma((Z // 2, 2)),
            dma((Z // 2, 2)),
            dma((Z // 2, 2, 2)),
            dma((pairs, 2)),
            dma((pairs, 2)),
        ],
        compiler_params=pltpu.CompilerParams(
            collective_id=0, has_side_effects=True, vmem_limit_bytes=40 * 1024 * 1024
        ),
        cost_estimate=pl.CostEstimate(flops=flops, bytes_accessed=4 << 20, transcendentals=0),
    )(
        target_q,
        target_kv,
        doc_kv,
        doc_lengths,
        segment_ids.reshape(ndoc, rows),
        out_weight,
    )


def solution(mesh):
    ndoc, nhead = mesh.shape["doc"], mesh.shape["head"]
    placed = (
        P("doc", "head"),
        P("doc", "head"),
        P("doc", None, "head"),
        P(),
        P(),
        P("head", "doc"),
    )
    return jax.shard_map(
        lambda *args: body(*args, ndoc, nhead),
        mesh=mesh,
        in_specs=placed,
        out_specs=P("head", "doc"),
        check_vma=False,
    )
```

```python
import math

import jax
import jax.numpy as jnp
from jax import lax
from jax.experimental import pallas as pl
from jax.experimental.pallas import tpu as pltpu
from jax.sharding import PartitionSpec as P

MASKED = -1e30
F32 = jnp.float32
BF16 = jnp.bfloat16


def ordered(pos, count, k):
    right = count - 1 - pos
    both = jnp.minimum(pos, right)
    near = jnp.where(k % 2 == 1, (k + 1) // 2, -(k // 2))
    far = jnp.where(right > pos, k - both, both - k)
    return pos + jnp.where(k <= 2 * both, near, far)


def kernel(
    ndoc,
    nhead,
    q_in,
    tkv_in,
    dkv_in,
    len_in,
    seg_in,
    w_ref,
    out_ref,
    len_ref,
    seg_ref,
    s_in,
    kv,
    tkv,
    wbuf,
    qbuf,
    m_s,
    l_s,
    acc_s,
    att,
    abuf,
    own,
    sbuf,
    rbuf,
    s_z,
    s_y,
    s_sib,
    r_doc,
    r_sib,
    s_t,
    r_t,
    s_w,
    r_w,
    l_w,
    s_a,
    s_az,
    s_ay,
    r_a,
    s_p,
    r_p,
):
    rows, cols = q_in.shape
    hd = tkv_in.shape[1]
    heads = cols // hd
    Z = ndoc // 2
    PAIRS = nhead // 2
    me = lax.axis_index("doc")
    hi = lax.axis_index("head")
    zi, y = me // 2, me % 2
    p, c = hi // 2, hi % 2
    sib = 2 * p + 1 - c
    ynb = 2 * zi + 1 - y
    t = zi % 2
    owner = 2 * p + t
    has_prev, has_next = me > 0, me < ndoc - 1
    coef = math.log2(math.e) / math.sqrt(hd)

    def rc(src, dst, ss, rs, doc, head):
        return pltpu.make_async_remote_copy(
            src_ref=src,
            dst_ref=dst,
            send_sem=ss,
            recv_sem=rs,
            device_id={"doc": doc, "head": head},
            device_id_type=pl.DeviceIdType.MESH,
        )

    load_doc = pltpu.make_async_copy(dkv_in.at[0], kv.at[c, me], s_in.at[0])
    load_tgt = pltpu.make_async_copy(tkv_in, tkv.at[c, pl.ds(rows, rows)], s_in.at[1])
    loads = [
        pltpu.make_async_copy(
            q_in.at[:, pl.ds(j * hd, hd)], qbuf.at[pl.ds(j * rows, rows)], s_in.at[4 + j]
        )
        for j in range(heads)
    ]
    loads.append(pltpu.make_async_copy(len_in, len_ref, s_in.at[2]))
    loads.append(pltpu.make_async_copy(seg_in, seg_ref, s_in.at[3]))
    w_local = pltpu.make_async_copy(w_ref, wbuf.at[c], l_w)
    for load in [load_doc, load_tgt] + loads + [w_local]:
        load.start()

    barrier = pltpu.get_barrier_semaphore()

    def greet(doc, head):
        pl.semaphore_signal(
            barrier, inc=1, device_id={"doc": doc, "head": head}, device_id_type=pl.DeviceIdType.MESH
        )

    diag = jnp.where(y == 1, me + 1, me - 1)
    has_diag = ((y == 1) & has_next) | ((y == 0) & has_prev)
    greet(me, sib)
    for core in range(2):
        greet(ynb, 2 * p + core)

        for k in range(1, Z):
            greet(2 * ((zi + k) % Z) + y, 2 * p + core)

        @pl.when(has_diag)
        def _():
            greet(diag, 2 * p + core)

    for k in range(1, PAIRS):
        greet(me, 2 * ((p + k) % PAIRS) + c)
    pl.semaphore_wait(barrier, 2 * Z + PAIRS + 2 * has_diag.astype(jnp.int32))

    def send_z(z):
        return rc(own_block, kv.at[c, me], s_z.at[z], r_doc.at[me], 2 * z + y, hi)

    def at_distance(k, act):
        pl.when(zi + k < Z)(lambda: act(zi + k))
        pl.when(zi - k >= 0)(lambda: act(zi - k))

    def advance(k, copy):
        at_distance(k, lambda z: copy(z).wait_send())
        at_distance(k + 1, lambda z: copy(z).start())

    def send_y(src, doc):
        return rc(src, kv.at[c, doc], s_y.at[doc], r_doc.at[doc], ynb, hi)

    def send_sib(src, doc):
        return rc(src, kv.at[c, doc], s_sib.at[doc], r_sib.at[doc], me, sib)

    own_block, tkv_ref = kv.at[c, me], tkv.at[c, pl.ds(rows, rows)]
    load_doc.wait()
    load_tgt.wait()
    t_own = rc(tkv_ref, tkv.at[c, pl.ds(rows, rows)], s_t.at[0], r_t.at[1], me, sib)
    t_next = [
        rc(tkv_ref, tkv.at[c, pl.ds(0, rows)], s_t.at[1], r_t.at[2], me + 1, hi),
        rc(tkv_ref, tkv.at[c, pl.ds(0, rows)], s_t.at[2], r_t.at[0], me + 1, sib),
    ]
    send_y(own_block, me).start()
    at_distance(1, lambda z: send_z(z).start())
    send_sib(own_block, me).start()
    t_own.start()

    @pl.when(has_next)
    def _():
        t_next[0].start()
        t_next[1].start()

    w_remote = rc(w_ref, wbuf.at[c], s_w, r_w, me, sib)
    w_remote.start()

    @pl.when(me == 0)
    def _():
        tkv[:, pl.ds(0, rows)] = jnp.zeros((2, rows, hd), BF16)

    def attend(keys, values, mask_of):
        half = cols // 2
        for part in range(2):
            at = slice(part * half, (part + 1) * half)
            scores = lax.dot_general(
                keys, qbuf[at], (((1,), (1,)), ((), ())), preferred_element_type=F32
            )
            scores = jnp.where(mask_of(half), scores, MASKED)
            before = m_s[:, at]
            high = jnp.maximum(jnp.max(scores, axis=0, keepdims=True), before)
            weights = jnp.exp2((scores - high) * coef)
            blended = lax.dot_general(
                values,
                weights.astype(BF16),
                (((0,), (0,)), ((), ())),
                preferred_element_type=F32,
            )
            factor = jnp.exp2((before - high) * coef)
            m_s[:, at] = high
            l_s[:, at] = jnp.sum(weights, axis=0, keepdims=True) + factor * l_s[:, at]
            acc_s[:, at] = blended + factor * acc_s[:, at]

    for load in loads:
        load.wait()
    m_s[...] = jnp.full_like(m_s, MASKED)
    l_s[...] = jnp.zeros_like(l_s)
    acc_s[...] = jnp.zeros_like(acc_s)

    def attend_doc(doc):
        send_sib(own_block, doc).wait_recv()
        keys = kv[0, doc]
        length = len_ref[doc]

        def mask_of(n):
            return lax.broadcasted_iota(jnp.int32, (keys.shape[0], n), 0) < length

        attend(keys, kv[1, doc], mask_of)

    def own_step(i, _):
        @pl.when(i < Z)
        def _():
            advance(i, send_z)
            z = ordered(zi, Z, i)
            doc = 2 * z + y
            block = kv.at[c, doc]
            send_y(own_block, doc).wait_recv()
            send_y(block, doc).start()
            send_sib(block, doc).start()

        attend_doc(2 * ordered(zi, Z, i - 1) + y)
        return 0

    def other_step(i, _):
        @pl.when(i < Z)
        def _():
            doc = 2 * ordered(zi, Z, i) + 1 - y
            send_y(own_block, doc).wait_recv()
            send_sib(kv.at[c, doc], doc).start()

        @pl.when(i > 0)
        def _():
            attend_doc(2 * ordered(zi, Z, i - 1) + 1 - y)

        return 0

    lax.fori_loop(1, Z + 1, own_step, 0)

    own_row = seg_ref[pl.ds(me, 1), :]
    prev_row = seg_ref[pl.ds(jnp.maximum(me - 1, 0), 1), :]

    def column(row):
        return jnp.broadcast_to(row.astype(F32), (rows, rows)).T

    own_col, prev_col = column(own_row), column(prev_row)
    own_rowf = jnp.broadcast_to(own_row.astype(F32), (rows, rows))
    key_pos = lax.broadcasted_iota(jnp.int32, (rows, rows), 0)
    row_pos = lax.broadcasted_iota(jnp.int32, (rows, rows), 1)
    prev_mask = jnp.where(has_prev, (prev_col == own_rowf).astype(F32), 0.0)
    own_mask = jnp.where((own_col == own_rowf) & (key_pos <= row_pos), 1.0, 0.0)
    tmask = jnp.concatenate([prev_mask, own_mask], axis=0)

    t_own.wait_recv()

    @pl.when(has_prev)
    def _():
        t_next[0].wait_recv()
        t_next[1].wait_recv()

    attend(
        tkv[0],
        tkv[1],
        lambda n: jnp.concatenate([tmask] * (n // rows), axis=1) > 0.5,
    )

    lax.fori_loop(0, Z + 1, other_step, 0)

    for j in range(heads):
        at = slice(j * rows, (j + 1) * rows)
        att[:, at] = (acc_s[:, at] / l_s[:, at]).T.astype(BF16)

    def unit(z, yy, half):
        return abuf.at[z // 2, yy, half]

    a_sib = rc(att, unit(zi, y, c), s_a.at[0], r_a.at[zi // 2, y, c], me, sib)

    def a_z(z):
        return rc(att, unit(zi, y, c), s_az.at[z], r_a.at[zi // 2, y, c], 2 * z + y, owner)

    a_y = rc(att, unit(zi, y, c), s_a.at[1], r_a.at[zi // 2, y, c], ynb, owner)
    a_y.start()
    for k in range(Z - 1, 0, -1):
        at_distance(k, lambda z: a_z(z).start())
    pl.when(t != c)(lambda: a_sib.start())

    @pl.when(t == c)
    def _():
        abuf[zi // 2, y, c] = att[...]

    w_local.wait()
    w_remote.wait_recv()

    def fwd(z, half):
        block = unit(z, y, half)
        return rc(block, block, s_ay.at[z // 2, half], r_a.at[z // 2, y, half], ynb, hi)

    def arrived(z, yy, half):
        rc(
            unit(z, yy, half), unit(z, yy, half), s_a.at[0], r_a.at[z // 2, yy, half], ynb, hi
        ).wait_recv()

    def part_copy(z, yy):
        return rc(sbuf.at[z // 2, yy], rbuf.at[p, yy], s_p.at[z // 2, yy], r_p.at[p, yy], me, z)

    def project(z, yy):
        part = jnp.dot(abuf[z // 2, yy, 0], wbuf[0], preferred_element_type=F32)
        part = part + jnp.dot(abuf[z // 2, yy, 1], wbuf[1], preferred_element_type=F32)
        sbuf[z // 2, yy] = part.astype(BF16)
        part_copy(z, yy).start()

    def place(k):
        return 2 * ordered(zi // 2, Z // 2, k) + c

    def own_rows(k, _):
        z = 2 * ((p + 1 + k) % PAIRS) + c

        @pl.when(z == zi)
        def _():
            arrived(z, y, 1 - c)

        for half in range(2):

            @pl.when(z != zi)
            def _():
                arrived(z, y, half)
                fwd(z, half).start()

        pl.when(z // 2 != p)(lambda: project(z, y))
        return 0

    def other_rows(k, _):
        z = 2 * ((p + k) % PAIRS) + c
        arrived(z, 1 - y, 0)
        arrived(z, 1 - y, 1)
        project(z, 1 - y)
        return 0

    lax.fori_loop(0, Z // 2, own_rows, 0)
    lax.fori_loop(1, PAIRS, other_rows, 0)
    arrived(2 * p + c, 1 - y, 0)
    arrived(2 * p + c, 1 - y, 1)
    own[...] = jnp.dot(
        abuf[p, :, 0].reshape(2 * rows, cols), wbuf[0], preferred_element_type=F32
    ) + jnp.dot(abuf[p, :, 1].reshape(2 * rows, cols), wbuf[1], preferred_element_type=F32)

    def add_in(k, _):
        src = (p + k) % PAIRS
        for yy in range(2):
            rc(
                sbuf.at[src, yy],
                rbuf.at[src, yy],
                s_p.at[src, yy],
                r_p.at[src, yy],
                me,
                2 * src + c,
            ).wait_recv()
            at = slice(yy * rows, (yy + 1) * rows)
            total = own[at] + rbuf[src, yy].astype(F32)
            if PAIRS == 2:
                out_ref[at] = total.astype(BF16)
            else:
                own[at] = total
        return 0

    if PAIRS == 2:
        add_in(1, 0)
    else:
        lax.fori_loop(1, PAIRS, add_in, 0)
        out_ref[...] = own[...].astype(BF16)

    t_own.wait_send()

    @pl.when(has_next)
    def _():
        t_next[0].wait_send()
        t_next[1].wait_send()

    w_remote.wait_send()

    def drain(z, _):
        doc = 2 * z + y
        send_y(own_block, doc).wait_send()
        send_sib(own_block, doc).wait_send()
        send_sib(own_block, 2 * z + 1 - y).wait_send()


        @pl.when(z % 2 == c)
        def _():
            for half in range(2):
                pl.when(z != zi)(lambda: fwd(z, half).wait_send())

            @pl.when(z // 2 != p)
            def _():
                for yy in range(2):
                    part_copy(z, yy).wait_send()

        return 0

    lax.fori_loop(0, Z, drain, 0)
    for k in range(1, Z):
        at_distance(k, lambda z: a_z(z).wait_send())
    a_y.wait_send()
    pl.when(t != c)(lambda: a_sib.wait_send())


def body(target_q, target_kv, doc_kv, doc_lengths, segment_ids, out_weight, ndoc, nhead):
    rows, cols = target_q.shape
    hd = target_kv.shape[1]
    slots = doc_kv.shape[1]
    wide = out_weight.shape[1]
    Z, pairs = ndoc // 2, nhead // 2
    vmem = pl.BlockSpec(memory_space=pltpu.VMEM)
    dma = pltpu.SemaphoreType.DMA
    flops = 4 * rows * cols * (ndoc * slots + 2 * rows) + 2 * ndoc * rows * cols * wide
    return pl.pallas_call(
        lambda *refs: kernel(ndoc, nhead, *refs),
        out_shape=jax.ShapeDtypeStruct((2 * rows, wide), BF16),
        in_specs=[pl.BlockSpec(memory_space=pltpu.HBM)] * 6,
        out_specs=vmem,
        scratch_shapes=[
            pltpu.SMEM((ndoc,), jnp.int32),
            pltpu.VMEM((ndoc, rows), jnp.int32),
            dma((4 + cols // hd,)),
            pltpu.VMEM((2, ndoc, slots, hd), BF16),
            pltpu.VMEM((2, 2 * rows, hd), BF16),
            pltpu.VMEM((2, cols, wide), BF16),
            pltpu.VMEM((cols // hd * rows, hd), BF16),
            pltpu.VMEM((1, cols // hd * rows), F32),
            pltpu.VMEM((1, cols // hd * rows), F32),
            pltpu.VMEM((hd, cols // hd * rows), F32),
            pltpu.VMEM((rows, cols), BF16),
            pltpu.VMEM((Z // 2, 2, 2, rows, cols), BF16),
            pltpu.VMEM((2 * rows, wide), F32),
            pltpu.VMEM((pairs, 2, rows, wide), BF16),
            pltpu.VMEM((pairs, 2, rows, wide), BF16),
            dma((Z,)),
            dma((ndoc,)),
            dma((ndoc,)),
            dma((ndoc,)),
            dma((ndoc,)),
            dma((3,)),
            dma((3,)),
            dma,
            dma,
            dma,
            dma((2,)),
            dma((Z,)),
            dma((Z // 2, 2)),
            dma((Z // 2, 2, 2)),
            dma((pairs, 2)),
            dma((pairs, 2)),
        ],
        compiler_params=pltpu.CompilerParams(
            collective_id=0, has_side_effects=True, vmem_limit_bytes=(64 << 20) - (1 << 16)
        ),
        cost_estimate=pl.CostEstimate(flops=flops, bytes_accessed=4 << 20, transcendentals=0),
    )(
        target_q,
        target_kv,
        doc_kv,
        doc_lengths,
        segment_ids.reshape(ndoc, rows),
        out_weight,
    )


def solution(mesh):
    ndoc, nhead = mesh.shape["doc"], mesh.shape["head"]
    placed = (
        P("doc", "head"),
        P("doc", "head"),
        P("doc", None, "head"),
        P(),
        P(),
        P("head", "doc"),
    )
    return jax.shard_map(
        lambda *args: body(*args, ndoc, nhead),
        mesh=mesh,
        in_specs=placed,
        out_specs=P("head", "doc"),
        check_vma=False,
    )
```

```python
import itertools
import math

import jax
import jax.numpy as jnp
from jax import lax
from jax.experimental import pallas as pl
from jax.experimental.pallas import tpu as pltpu
from jax.sharding import PartitionSpec as P

MASKED = -1e30
PIECES = 2
F32 = jnp.float32
BF16 = jnp.bfloat16


def ordered(pos, count, k):
    right = count - 1 - pos
    both = jnp.minimum(pos, right)
    near = jnp.where(k % 2 == 1, (k + 1) // 2, -(k // 2))
    far = jnp.where(right > pos, k - both, both - k)
    return pos + jnp.where(k <= 2 * both, near, far)


def kernel(
    ndoc,
    nhead,
    q_in,
    tkv_in,
    dkv_in,
    len_in,
    seg_in,
    w_ref,
    out_ref,
    len_ref,
    seg_ref,
    s_in,
    kv,
    tkv,
    wbuf,
    qbuf,
    m_s,
    l_s,
    acc_s,
    att,
    abuf,
    own,
    sbuf,
    rbuf,
    s_z,
    s_y,
    s_sib,
    r_doc,
    r_sib,
    s_t,
    r_t,
    s_w,
    r_w,
    l_w,
    s_a,
    s_az,
    s_ay,
    r_a,
    s_p,
    r_p,
):
    rows, cols = q_in.shape
    hd = tkv_in.shape[1]
    heads = cols // hd
    piece = rows // PIECES
    Z = ndoc // 2
    PAIRS = nhead // 2
    me = lax.axis_index("doc")
    hi = lax.axis_index("head")
    zi, y = me // 2, me % 2
    p, c = hi // 2, hi % 2
    sib = 2 * p + 1 - c
    ynb = 2 * zi + 1 - y
    t = zi % 2
    owner = 2 * p + t
    has_prev, has_next = me > 0, me < ndoc - 1
    coef = math.log2(math.e) / math.sqrt(hd)

    def rc(src, dst, ss, rs, doc, head):
        return pltpu.make_async_remote_copy(
            src_ref=src,
            dst_ref=dst,
            send_sem=ss,
            recv_sem=rs,
            device_id={"doc": doc, "head": head},
            device_id_type=pl.DeviceIdType.MESH,
        )

    load_doc = pltpu.make_async_copy(dkv_in.at[0], kv.at[c, me], s_in.at[0])
    load_tgt = pltpu.make_async_copy(tkv_in, tkv.at[c, pl.ds(rows, rows)], s_in.at[1])
    loads = [
        pltpu.make_async_copy(
            q_in.at[:, pl.ds(j * hd, hd)], qbuf.at[pl.ds(j * rows, rows)], s_in.at[4 + j]
        )
        for j in range(heads)
    ]
    loads.append(pltpu.make_async_copy(len_in, len_ref, s_in.at[2]))
    loads.append(pltpu.make_async_copy(seg_in, seg_ref, s_in.at[3]))
    w_local = pltpu.make_async_copy(w_ref, wbuf.at[c], l_w)
    for load in [load_doc, load_tgt] + loads + [w_local]:
        load.start()

    barrier = pltpu.get_barrier_semaphore()

    def greet(doc, head):
        pl.semaphore_signal(
            barrier, inc=1, device_id={"doc": doc, "head": head}, device_id_type=pl.DeviceIdType.MESH
        )

    diag = jnp.where(y == 1, me + 1, me - 1)
    has_diag = ((y == 1) & has_next) | ((y == 0) & has_prev)
    greet(me, sib)
    for core in range(2):
        greet(ynb, 2 * p + core)

        for k in range(1, Z):
            greet(2 * ((zi + k) % Z) + y, 2 * p + core)

        @pl.when(has_diag)
        def _():
            greet(diag, 2 * p + core)

    for k in range(1, PAIRS):
        greet(me, 2 * ((p + k) % PAIRS) + c)
    pl.semaphore_wait(barrier, 2 * Z + PAIRS + 2 * has_diag.astype(jnp.int32))

    def send_z(z):
        return rc(own_block, kv.at[c, me], s_z.at[z], r_doc.at[me], 2 * z + y, hi)

    def at_distance(k, act):
        pl.when(zi + k < Z)(lambda: act(zi + k))
        pl.when(zi - k >= 0)(lambda: act(zi - k))

    def advance(k, copy):
        at_distance(k, lambda z: copy(z).wait_send())
        at_distance(k + 1, lambda z: copy(z).start())

    def send_y(src, doc):
        return rc(src, kv.at[c, doc], s_y.at[doc], r_doc.at[doc], ynb, hi)

    def send_sib(src, doc):
        return rc(src, kv.at[c, doc], s_sib.at[doc], r_sib.at[doc], me, sib)

    own_block, tkv_ref = kv.at[c, me], tkv.at[c, pl.ds(rows, rows)]
    load_doc.wait()
    load_tgt.wait()
    t_own = rc(tkv_ref, tkv.at[c, pl.ds(rows, rows)], s_t.at[0], r_t.at[1], me, sib)
    t_next = [
        rc(tkv_ref, tkv.at[c, pl.ds(0, rows)], s_t.at[1], r_t.at[2], me + 1, hi),
        rc(tkv_ref, tkv.at[c, pl.ds(0, rows)], s_t.at[2], r_t.at[0], me + 1, sib),
    ]
    send_y(own_block, me).start()
    at_distance(1, lambda z: send_z(z).start())
    send_sib(own_block, me).start()
    t_own.start()

    @pl.when(has_next)
    def _():
        t_next[0].start()
        t_next[1].start()

    w_remote = rc(w_ref, wbuf.at[c], s_w, r_w, me, sib)
    w_remote.start()

    @pl.when(me == 0)
    def _():
        tkv[:, pl.ds(0, rows)] = jnp.zeros((2, rows, hd), BF16)

    def attend(keys, values, mask_of):
        half = cols // 2
        for part in range(2):
            at = slice(part * half, (part + 1) * half)
            scores = lax.dot_general(
                keys, qbuf[at], (((1,), (1,)), ((), ())), preferred_element_type=F32
            )
            scores = jnp.where(mask_of(half), scores, MASKED)
            before = m_s[:, at]
            high = jnp.maximum(jnp.max(scores, axis=0, keepdims=True), before)
            weights = jnp.exp2((scores - high) * coef)
            blended = lax.dot_general(
                values,
                weights.astype(BF16),
                (((0,), (0,)), ((), ())),
                preferred_element_type=F32,
            )
            factor = jnp.exp2((before - high) * coef)
            m_s[:, at] = high
            l_s[:, at] = jnp.sum(weights, axis=0, keepdims=True) + factor * l_s[:, at]
            acc_s[:, at] = blended + factor * acc_s[:, at]

    for load in loads:
        load.wait()
    m_s[...] = jnp.full_like(m_s, MASKED)
    l_s[...] = jnp.zeros_like(l_s)
    acc_s[...] = jnp.zeros_like(acc_s)

    def attend_doc(doc):
        send_sib(own_block, doc).wait_recv()
        keys = kv[0, doc]
        length = len_ref[doc]

        def mask_of(n):
            return lax.broadcasted_iota(jnp.int32, (keys.shape[0], n), 0) < length

        attend(keys, kv[1, doc], mask_of)

    def own_step(i, _):
        @pl.when(i < Z)
        def _():
            advance(i, send_z)
            z = ordered(zi, Z, i)
            doc = 2 * z + y
            block = kv.at[c, doc]
            send_y(own_block, doc).wait_recv()
            send_y(block, doc).start()
            send_sib(block, doc).start()

        attend_doc(2 * ordered(zi, Z, i - 1) + y)
        return 0

    def other_step(i, _):
        @pl.when(i < Z)
        def _():
            doc = 2 * ordered(zi, Z, i) + 1 - y
            send_y(own_block, doc).wait_recv()
            send_sib(kv.at[c, doc], doc).start()

        @pl.when(i > 0)
        def _():
            attend_doc(2 * ordered(zi, Z, i - 1) + 1 - y)

        return 0

    lax.fori_loop(1, Z + 1, own_step, 0)

    own_row = seg_ref[pl.ds(me, 1), :]
    prev_row = seg_ref[pl.ds(jnp.maximum(me - 1, 0), 1), :]

    def column(row):
        return jnp.broadcast_to(row.astype(F32), (rows, rows)).T

    own_col, prev_col = column(own_row), column(prev_row)
    own_rowf = jnp.broadcast_to(own_row.astype(F32), (rows, rows))
    key_pos = lax.broadcasted_iota(jnp.int32, (rows, rows), 0)
    row_pos = lax.broadcasted_iota(jnp.int32, (rows, rows), 1)
    prev_mask = jnp.where(has_prev, (prev_col == own_rowf).astype(F32), 0.0)
    own_mask = jnp.where((own_col == own_rowf) & (key_pos <= row_pos), 1.0, 0.0)
    tmask = jnp.concatenate([prev_mask, own_mask], axis=0)

    t_own.wait_recv()

    @pl.when(has_prev)
    def _():
        t_next[0].wait_recv()
        t_next[1].wait_recv()

    attend(
        tkv[0],
        tkv[1],
        lambda n: jnp.concatenate([tmask] * (n // rows), axis=1) > 0.5,
    )

    lax.fori_loop(0, Z + 1, other_step, 0)

    for j in range(heads):
        at = slice(j * rows, (j + 1) * rows)
        att[:, at] = (acc_s[:, at] / l_s[:, at]).T.astype(BF16)

    def unit(z, yy, half, r):
        return abuf.at[z // 2, yy, half, pl.ds(r * piece, piece)]

    def a_copy(r, sem, doc, head):
        return rc(
            att.at[pl.ds(r * piece, piece)],
            unit(zi, y, c, r),
            sem,
            r_a.at[zi // 2, y, c, r],
            doc,
            head,
        )

    def a_sib(r):
        return a_copy(r, s_a.at[0, r], me, sib)

    def a_y(r):
        return a_copy(r, s_a.at[1, r], ynb, owner)

    def a_z(z, r):
        return a_copy(r, s_az.at[z, r], 2 * z + y, owner)

    for r in range(PIECES):
        a_y(r).start()
        for k in range(Z - 1, 0, -1):
            at_distance(k, lambda z: a_z(z, r).start())
        pl.when(t != c)(lambda: a_sib(r).start())

    @pl.when(t == c)
    def _():
        abuf[zi // 2, y, c] = att[...]

    w_local.wait()
    w_remote.wait_recv()

    def fwd(z, half, r):
        block = unit(z, y, half, r)
        return rc(block, block, s_ay.at[z // 2, half, r], r_a.at[z // 2, y, half, r], ynb, hi)

    def arrived(z, yy, half, r):
        block = unit(z, yy, half, r)
        rc(block, block, s_a.at[0, r], r_a.at[z // 2, yy, half, r], ynb, hi).wait_recv()

    def part_copy(src, slot, yy, r, z):
        at = pl.ds(r * piece, piece)
        return rc(
            sbuf.at[src, yy, at],
            rbuf.at[slot, yy, at],
            s_p.at[src, yy, r],
            r_p.at[slot, yy, r],
            me,
            z,
        )

    def project(z, yy, r):
        at = slice(r * piece, (r + 1) * piece)
        part = jnp.dot(abuf[z // 2, yy, 0, at], wbuf[0], preferred_element_type=F32)
        part = part + jnp.dot(abuf[z // 2, yy, 1, at], wbuf[1], preferred_element_type=F32)
        sbuf[z // 2, yy, at] = part.astype(BF16)
        part_copy(z // 2, p, yy, r, z).start()

    def own_rows(k, _):
        z = 2 * ((p + 1 + k) % PAIRS) + c

        for r in range(PIECES):

            @pl.when(z == zi)
            def _():
                arrived(z, y, 1 - c, r)

            for half in range(2):

                @pl.when(z != zi)
                def _():
                    arrived(z, y, half, r)
                    fwd(z, half, r).start()

            pl.when(z // 2 != p)(lambda: project(z, y, r))
        return 0

    def other_rows(k, _):
        z = 2 * ((p + k) % PAIRS) + c
        for r in range(PIECES):
            arrived(z, 1 - y, 0, r)
            arrived(z, 1 - y, 1, r)
            project(z, 1 - y, r)
        return 0

    lax.fori_loop(0, Z // 2, own_rows, 0)
    lax.fori_loop(1, PAIRS, other_rows, 0)
    for r in range(PIECES):
        arrived(2 * p + c, 1 - y, 0, r)
        arrived(2 * p + c, 1 - y, 1, r)
    own[...] = jnp.dot(
        abuf[p, :, 0].reshape(2 * rows, cols), wbuf[0], preferred_element_type=F32
    ) + jnp.dot(abuf[p, :, 1].reshape(2 * rows, cols), wbuf[1], preferred_element_type=F32)

    def add_in(k, _):
        src = (p + k) % PAIRS
        for yy, r in itertools.product(range(2), range(PIECES)):
            part_copy(src, src, yy, r, 2 * src + c).wait_recv()
            low = yy * rows + r * piece
            at = slice(low, low + piece)
            total = own[at] + rbuf[src, yy, r * piece : (r + 1) * piece].astype(F32)
            if PAIRS == 2:
                out_ref[at] = total.astype(BF16)
            else:
                own[at] = total
        return 0

    if PAIRS == 2:
        add_in(1, 0)
    else:
        lax.fori_loop(1, PAIRS, add_in, 0)
        out_ref[...] = own[...].astype(BF16)

    t_own.wait_send()

    @pl.when(has_next)
    def _():
        t_next[0].wait_send()
        t_next[1].wait_send()

    w_remote.wait_send()

    def drain(z, _):
        doc = 2 * z + y
        send_y(own_block, doc).wait_send()
        send_sib(own_block, doc).wait_send()
        send_sib(own_block, 2 * z + 1 - y).wait_send()


        @pl.when(z % 2 == c)
        def _():
            for half, r in itertools.product(range(2), range(PIECES)):
                pl.when(z != zi)(lambda: fwd(z, half, r).wait_send())

            @pl.when(z // 2 != p)
            def _():
                for yy, r in itertools.product(range(2), range(PIECES)):
                    part_copy(z // 2, p, yy, r, z).wait_send()

        return 0

    lax.fori_loop(0, Z, drain, 0)
    for r in range(PIECES):
        for k in range(1, Z):
            at_distance(k, lambda z: a_z(z, r).wait_send())
        a_y(r).wait_send()
        pl.when(t != c)(lambda: a_sib(r).wait_send())


def body(target_q, target_kv, doc_kv, doc_lengths, segment_ids, out_weight, ndoc, nhead):
    rows, cols = target_q.shape
    hd = target_kv.shape[1]
    slots = doc_kv.shape[1]
    wide = out_weight.shape[1]
    Z, pairs = ndoc // 2, nhead // 2
    vmem = pl.BlockSpec(memory_space=pltpu.VMEM)
    dma = pltpu.SemaphoreType.DMA
    flops = 4 * rows * cols * (ndoc * slots + 2 * rows) + 2 * ndoc * rows * cols * wide
    return pl.pallas_call(
        lambda *refs: kernel(ndoc, nhead, *refs),
        out_shape=jax.ShapeDtypeStruct((2 * rows, wide), BF16),
        in_specs=[pl.BlockSpec(memory_space=pltpu.HBM)] * 6,
        out_specs=vmem,
        scratch_shapes=[
            pltpu.SMEM((ndoc,), jnp.int32),
            pltpu.VMEM((ndoc, rows), jnp.int32),
            dma((4 + cols // hd,)),
            pltpu.VMEM((2, ndoc, slots, hd), BF16),
            pltpu.VMEM((2, 2 * rows, hd), BF16),
            pltpu.VMEM((2, cols, wide), BF16),
            pltpu.VMEM((cols // hd * rows, hd), BF16),
            pltpu.VMEM((1, cols // hd * rows), F32),
            pltpu.VMEM((1, cols // hd * rows), F32),
            pltpu.VMEM((hd, cols // hd * rows), F32),
            pltpu.VMEM((rows, cols), BF16),
            pltpu.VMEM((Z // 2, 2, 2, rows, cols), BF16),
            pltpu.VMEM((2 * rows, wide), F32),
            pltpu.VMEM((pairs, 2, rows, wide), BF16),
            pltpu.VMEM((pairs, 2, rows, wide), BF16),
            dma((Z,)),
            dma((ndoc,)),
            dma((ndoc,)),
            dma((ndoc,)),
            dma((ndoc,)),
            dma((3,)),
            dma((3,)),
            dma,
            dma,
            dma,
            dma((2, PIECES)),
            dma((Z, PIECES)),
            dma((Z // 2, 2, PIECES)),
            dma((Z // 2, 2, 2, PIECES)),
            dma((pairs, 2, PIECES)),
            dma((pairs, 2, PIECES)),
        ],
        compiler_params=pltpu.CompilerParams(
            collective_id=0, has_side_effects=True, vmem_limit_bytes=(64 << 20) - (1 << 16)
        ),
        cost_estimate=pl.CostEstimate(flops=flops, bytes_accessed=4 << 20, transcendentals=0),
    )(
        target_q,
        target_kv,
        doc_kv,
        doc_lengths,
        segment_ids.reshape(ndoc, rows),
        out_weight,
    )


def solution(mesh):
    ndoc, nhead = mesh.shape["doc"], mesh.shape["head"]
    placed = (
        P("doc", "head"),
        P("doc", "head"),
        P("doc", None, "head"),
        P(),
        P(),
        P("head", "doc"),
    )
    return jax.shard_map(
        lambda *args: body(*args, ndoc, nhead),
        mesh=mesh,
        in_specs=placed,
        out_specs=P("head", "doc"),
        check_vma=False,
    )
```
